512 devices in a mesh: dp: 64 (over y_hi, z, core), mp: 8 (over y_lo, x).
Axes of the slice: x: 4, y: 8 (y_hi: 4, y_lo: 2; y = y_hi * 2 + y_lo), z: 8, core: 2. Of those that a mesh axis runs over, the one named last changes fastest.
Arguments:
- spec_feat: bfloat16 [8192, 2048], P('dp', 'mp'), may hold values from -6 to 6
- pep_feat: bfloat16 [8192, 2048], P('dp', 'mp'), may hold values from -6 to 6
- w_spec: bfloat16 [2048, 768], P('mp'), may hold values from -0.125 to 0.125
- w_pep: bfloat16 [2048, 768], P('mp'), may hold values from -0.125 to 0.125
- teach_spec: bfloat16 [8192, 768], P('dp'), may hold values from -6 to 6
- teach_pep: bfloat16 [8192, 768], P(('dp', 'mp')), may hold values from -6 to 6
- exp_spec: int32 [768], replicated, may hold values from 6 to 8
- exp_pep: int32 [768], replicated, may hold values from 6 to 8
- positive: int32 [8192], P('dp'), may hold values from 0 to 8191
Outputs:
- spec_grad: float32 [8192, 768], P(('dp', 'mp'))
- pep_grad: float32 [8192, 768], P(('dp', 'mp'))
The draws below stay inside these ranges and needn't reach their ends.
All inputs are finite; a program needn't handle non-finite values.
Results may differ from the reference program's by a relative error of at most 0.0024.
Values may be sent and summed in bfloat16 or wider, within the bound.
No kernel may reach another device: no remote copies, remote signals or barrier semaphores. Data moves between devices by JAX's collectives and lax.ppermute only.
A program may use at most 64 MiB of HBM per device.

```python
import math
import jax
import jax.numpy as jnp
from jax import lax

F = 2048
E = 768
PAIRS = 8192


def plant(values, own_key, low, largest):
    dims = values.shape
    spot = [jax.random.randint(jax.random.fold_in(own_key, axis), (), 0, dims[axis]) for axis in range(len(dims))]
    values = values.at[tuple(spot)].set(low)
    longest = dims.index(max(dims))
    spot[longest] = (spot[longest] + 1) % dims[longest]
    return values.at[tuple(spot)].set(largest)


def steps_of(own_key, shape, shards, low, top_value):
    loudness = 1.0
    for position, shards_of in shards:
        draws = jax.random.uniform(jax.random.fold_in(jax.random.fold_in(own_key, 6), position), (shards_of,), jnp.float32, low / len(shards), top_value / len(shards))
        loudness = loudness * jnp.repeat(jnp.exp(draws), shape[position] // shards_of).reshape((-1,) + (1,) * (len(shape) - 1 - position))
    return loudness


def bell_draw(own_key, dims, scale, limit, cuts=(), kind=jnp.bfloat16):
    values = jax.random.normal(own_key, dims, jnp.float32) * scale
    if len(cuts) > 0:
        values = steps_of(own_key, dims, cuts, -0.22, 0.18) * values
    return jnp.clip(values, min=-limit, max=limit).astype(kind)


def setup_inputs(seed: int = 0) -> dict:
    splits = jax.random.split(jax.random.key(seed), 10)
    spec_feat = bell_draw(splits[0], (PAIRS, F), 1.0, 6.0, ((0, 64), (1, 8)))
    pep_feat = bell_draw(splits[1], (PAIRS, F), 1.0, 6.0, ((0, 64), (1, 8)))
    w_spec = bell_draw(splits[2], (F, E), F ** -0.5, 0.125, ((0, 8),))
    w_pep = bell_draw(splits[3], (F, E), F ** -0.5, 0.125, ((0, 8),))
    teach_spec = bell_draw(splits[4], (PAIRS, E), 1.0, 6.0, ((0, 64),))
    teach_pep = bell_draw(splits[5], (PAIRS, E), 1.0, 6.0, ((0, 512),))
    exp_spec = plant(jax.random.randint(splits[6], (E,), 6, 9), jax.random.fold_in(splits[6], 1), 6, 8).astype(jnp.int32)
    exp_pep = plant(jax.random.randint(splits[7], (E,), 6, 9), jax.random.fold_in(splits[7], 1), 6, 8).astype(jnp.int32)
    positive = plant(jax.random.randint(splits[8], (PAIRS,), 0, PAIRS), jax.random.fold_in(splits[8], 1), 0, PAIRS - 1).astype(jnp.int32)
    return dict(spec_feat=spec_feat, pep_feat=pep_feat, w_spec=w_spec, w_pep=w_pep, teach_spec=teach_spec, teach_pep=teach_pep, exp_spec=exp_spec, exp_pep=exp_pep, positive=positive)


LOGIT_GAIN = 4.0
LOGIT_SHIFT = -2.0
CLIP_LEVELS = 127.0

def clip_channels(pre_proj, exponents):
    limits = CLIP_LEVELS * jnp.exp2(-exponents.astype(jnp.float32))
    return jnp.clip(pre_proj, -limits, limits).astype(jnp.bfloat16)

def reference(spec_feat, pep_feat, w_spec, w_pep, teach_spec, teach_pep, exp_spec, exp_pep, positive):
    spec_q = clip_channels(jnp.dot(spec_feat, w_spec, preferred_element_type=jnp.float32), exp_spec)
    pep_q = clip_channels(jnp.dot(pep_feat, w_pep, preferred_element_type=jnp.float32), exp_pep)
    width = spec_q.shape[1]
    factor = LOGIT_GAIN / math.sqrt(width)
    block = math.gcd(PAIRS, 512)
    blocks = PAIRS // block
    peptide_ids = jnp.arange(PAIRS, dtype=jnp.int32)
    inner = (((1,), (1,)), ((), ()))
    outer = (((0,), (0,)), ((), ()))

    def step(pep_acc, pieces):
        spec_block, teach_block, pos_block = pieces
        student = factor * lax.dot_general(spec_block, pep_q, inner, preferred_element_type=jnp.float32) + LOGIT_SHIFT
        teacher = factor * lax.dot_general(teach_block, teach_pep, inner, preferred_element_type=jnp.float32)
        hard = (pos_block[:, None] == peptide_ids[None, :]).astype(jnp.float32)
        target = 0.5 * hard + 0.5 * jax.nn.sigmoid(teacher)
        grads = (jax.nn.sigmoid(student) - target).astype(jnp.bfloat16)
        spec_block_grad = factor * jnp.dot(grads, pep_q, preferred_element_type=jnp.float32)
        pep_acc = pep_acc + lax.dot_general(grads, spec_block, outer, preferred_element_type=jnp.float32)
        return (pep_acc, spec_block_grad)
    pep_acc, spec_blocks = lax.scan(step, jnp.zeros((PAIRS, width), jnp.float32), (spec_q.reshape(blocks, block, width), teach_spec.reshape(blocks, block, width), positive.reshape(blocks, block)))
    return (spec_blocks.reshape(PAIRS, width), factor * pep_acc)
```

```python
import math

import numpy as np

import jax
import jax.numpy as jnp
from jax import lax
from jax.sharding import PartitionSpec as P

LOGIT_GAIN = 4.0
LOGIT_SHIFT = -2.0
CLIP_LEVELS = 127.0
AXES = ("dp", "mp")


def device_groups(mesh):
    flat = np.arange(mesh.shape["dp"] * mesh.shape["mp"]).reshape(4, 8, 2, 2, 2, 2)
    core_mp = flat.transpose(0, 1, 2, 3, 4, 5).reshape(32, 16)
    even = flat[:, :, 0]
    odd = flat[:, :, 1]
    spec_side = even.transpose(1, 3, 0, 2, 4).reshape(16, 16)
    pep_side = odd.transpose(0, 2, 4, 1, 3).reshape(16, 16)
    grid = np.concatenate([spec_side, pep_side], 0)
    pairs = [(int(a), int(b)) for a, b in zip(flat[:, :, 0].ravel(), flat[:, :, 1].ravel())]
    swap = pairs + [(b, a) for a, b in pairs]
    return core_mp.tolist(), grid.tolist(), swap


def body(groups, spec_feat, pep_feat, w_spec, w_pep, teach_spec, teach_pep, exp_spec, exp_pep, positive):
    core_mp, grid, swap = groups
    width = w_spec.shape[1]
    factor = LOGIT_GAIN / math.sqrt(width)
    rows = teach_pep.shape[0]
    dp_index = lax.axis_index("dp")
    mp_index = lax.axis_index("mp")
    even = dp_index % 2 == 0

    tags_spec = lax.dynamic_slice_in_dim(positive, mp_index * rows, rows)
    tags_pep = (dp_index * 8 + mp_index) * rows + jnp.arange(rows, dtype=jnp.int32)

    def with_tags(teach, tags):
        hi = (tags // 128).astype(jnp.bfloat16)[:, None]
        lo = (tags % 128).astype(jnp.bfloat16)[:, None]
        return jnp.concatenate([teach, hi, lo, jnp.zeros((rows, 126), jnp.bfloat16)], 1)

    t_spec = with_tags(lax.dynamic_slice_in_dim(teach_spec, mp_index * rows, rows), tags_spec)
    t_pep = with_tags(teach_pep, tags_pep)
    keep = jnp.where(even, t_spec, t_pep)
    got = lax.ppermute(jnp.where(even, t_pep, t_spec), AXES, swap)
    teach_rows = jnp.concatenate([jnp.where(even, keep, got), jnp.where(even, got, keep)], 0)

    part_spec = jnp.dot(spec_feat, w_spec, preferred_element_type=jnp.float32).astype(jnp.float16)
    part_pep = jnp.dot(pep_feat, w_pep, preferred_element_type=jnp.float32).astype(jnp.float16)
    parts = jnp.concatenate([part_spec.reshape(8, rows, width), part_pep.reshape(8, rows, width)], 0)
    parts = lax.all_to_all(parts, AXES, 0, 0, axis_index_groups=core_mp)
    sums = parts.reshape(2, 8, rows, width).astype(jnp.float32).sum(1).reshape(2 * rows, width)
    limits = CLIP_LEVELS * jnp.exp2(-jnp.where(even, exp_spec, exp_pep).astype(jnp.float32))
    q_rows = jnp.clip(sums, -limits, limits).astype(jnp.bfloat16)

    mine = jnp.concatenate([q_rows, teach_rows], 1)
    mine = lax.all_to_all(
        jnp.broadcast_to(mine[None], (16,) + mine.shape), AXES, 0, 0, axis_index_groups=grid
    ).reshape(16 * 2 * rows, -1)
    other = lax.ppermute(mine, AXES, swap)

    def unpack(block):
        tags = block[:, 2 * width : 2 * width + 2].astype(jnp.float32)
        return block[:, :width], block[:, width : 2 * width], 128.0 * tags[:, 0] + tags[:, 1]

    q_mine, t_mine, tag_mine = unpack(mine)
    q_other, t_other, tag_other = unpack(other)
    inner = (((1,), (1,)), ((), ()))
    student = factor * lax.dot_general(q_mine, q_other, inner, preferred_element_type=jnp.float32) + LOGIT_SHIFT
    teacher = factor * lax.dot_general(t_mine, t_other, inner, preferred_element_type=jnp.float32)
    hard = (tag_mine[:, None] == tag_other[None, :]).astype(jnp.float32)
    target = 0.5 * hard + 0.5 * jax.nn.sigmoid(teacher)
    grads = (jax.nn.sigmoid(student) - target).astype(jnp.bfloat16)
    acc = jnp.dot(grads, q_other, preferred_element_type=jnp.float32).astype(jnp.float16)
    acc = lax.all_to_all(acc.reshape(16, 2 * rows, width), AXES, 0, 0, axis_index_groups=grid)
    acc = factor * acc.astype(jnp.float32).sum(0)
    first, second = acc[:rows], acc[rows:]
    own = jnp.where(even, first, second)
    swapped = lax.ppermute(jnp.where(even, second, first), AXES, swap)
    return jnp.where(even, own, swapped), jnp.where(even, swapped, own)


def solution(mesh):
    groups = device_groups(mesh)

    def run(*args):
        return body(groups, *args)

    in_specs = (
        P("dp", "mp"),
        P("dp", "mp"),
        P("mp", None),
        P("mp", None),
        P("dp", None),
        P(("dp", "mp"), None),
        P(),
        P(),
        P("dp"),
    )
    out_specs = (P(("dp", "mp"), None), P(("dp", "mp"), None))
    return jax.shard_map(run, mesh=mesh, in_specs=in_specs, out_specs=out_specs, check_vma=False)
```

```python
import math

import numpy as np

import jax
import jax.numpy as jnp
from jax import lax
from jax.experimental import pallas as pl
from jax.experimental.pallas import tpu as pltpu
from jax.sharding import PartitionSpec as P

LOGIT_GAIN = 4.0
LOGIT_SHIFT = -2.0
CLIP_LEVELS = 127.0
AXES = ("dp", "mp")


def pair_kernel(factor, width, mine, other, out, held, sems):
    ahead = [
        pltpu.make_async_copy(other.at[:, cols], held.at[:, cols], sems.at[i])
        for i, cols in enumerate((pl.ds(width, width + 128), pl.ds(0, width)))
    ]
    for copy in ahead:
        copy.start()
    inner = (((1,), (1,)), ((), ()))
    size = mine.shape[0] // 2
    lane = lax.broadcasted_iota(jnp.int32, (8, 128), 1)
    weigh = jnp.where(lane == 0, 128.0, jnp.where(lane == 1, 1.0, 0.0)).astype(jnp.bfloat16)
    ahead[0].wait()
    tag_other = lax.dot_general(weigh, held[:, 2 * width :], inner, preferred_element_type=jnp.float32)[0:1]
    targets = []
    for start in (0, size):
        at = pl.ds(start, size)
        teacher = lax.dot_general(
            mine[at, width : 2 * width], held[:, width : 2 * width], inner, preferred_element_type=jnp.float32
        )
        tags = mine[at, 2 * width :].astype(jnp.float32)
        tag_mine = 128.0 * tags[:, 0:1] + tags[:, 1:2]
        hard = jnp.where(tag_mine == tag_other, 0.5, 0.0)
        targets.append(0.25 * jnp.tanh((0.5 * factor) * teacher) - 0.25 + hard)
    ahead[1].wait()
    for start, target in zip((0, size), targets):
        at = pl.ds(start, size)
        student = lax.dot_general(mine[at, :width], held[:, :width], inner, preferred_element_type=jnp.float32)
        grads = 0.5 * jnp.tanh((0.5 * factor) * student + 0.5 * LOGIT_SHIFT) - target
        out[at, :] = jnp.dot(grads.astype(jnp.bfloat16), held[:, :width], preferred_element_type=jnp.float32)


def pair_grads(mine, other, factor, width):
    return pl.pallas_call(
        lambda *refs: pair_kernel(factor, width, *refs),
        out_shape=jax.ShapeDtypeStruct((mine.shape[0], width), jnp.float32),
        in_specs=[pl.BlockSpec(memory_space=pltpu.VMEM), pl.BlockSpec(memory_space=pl.ANY)],
        out_specs=pl.BlockSpec(memory_space=pltpu.VMEM),
        scratch_shapes=[pltpu.VMEM(other.shape, other.dtype), pltpu.SemaphoreType.DMA((2,))],
        compiler_params=pltpu.CompilerParams(vmem_limit_bytes=32 * 2**20),
    )(mine, other)


def device_groups(mesh):
    flat = np.arange(mesh.shape["dp"] * mesh.shape["mp"]).reshape(4, 8, 2, 2, 4)
    core_mp = flat.reshape(32, 16)
    flat = flat[..., [0, 1, 3, 2]].reshape(4, 8, 2, 2, 2, 2)
    even = flat[:, :, 0]
    odd = flat[:, :, 1]
    spec_side = even.transpose(1, 3, 0, 2, 4).reshape(16, 16)
    pep_side = odd.transpose(0, 2, 4, 1, 3).reshape(16, 16)
    grid = np.concatenate([spec_side, pep_side], 0)
    pairs = [(int(a), int(b)) for a, b in zip(flat[:, :, 0].ravel(), flat[:, :, 1].ravel())]
    swap = pairs + [(b, a) for a, b in pairs]
    return core_mp.tolist(), grid.tolist(), [list(pair) for pair in pairs], swap


def body(groups, spec_feat, pep_feat, w_spec, w_pep, teach_spec, teach_pep, exp_spec, exp_pep, positive):
    core_mp, grid, pairs, swap = groups
    width = w_spec.shape[1]
    factor = LOGIT_GAIN / math.sqrt(width)
    rows = teach_pep.shape[0]
    dp_index = lax.axis_index("dp")
    mp_index = lax.axis_index("mp")
    even = dp_index % 2 == 0

    tags_spec = lax.dynamic_slice_in_dim(positive, mp_index * rows, rows)
    tags_pep = (dp_index * 8 + mp_index) * rows + jnp.arange(rows, dtype=jnp.int32)

    def with_tags(teach, tags):
        hi = (tags // 128).astype(jnp.bfloat16)[:, None]
        lo = (tags % 128).astype(jnp.bfloat16)[:, None]
        return jnp.concatenate([teach, hi, lo, jnp.zeros((rows, 126), jnp.bfloat16)], 1)

    t_spec = with_tags(lax.dynamic_slice_in_dim(teach_spec, mp_index * rows, rows), tags_spec)
    t_pep = with_tags(teach_pep, tags_pep)
    keep = jnp.where(even, t_spec, t_pep)
    got = lax.ppermute(jnp.where(even, t_pep, t_spec), AXES, swap)
    teach_rows = jnp.concatenate([jnp.where(even, keep, got), jnp.where(even, got, keep)], 0)

    part_spec = jnp.dot(spec_feat, w_spec, preferred_element_type=jnp.float32)
    part_pep = jnp.dot(pep_feat, w_pep, preferred_element_type=jnp.float32)
    part_spec, part_pep = lax.optimization_barrier((part_spec, part_pep))
    parts = jnp.concatenate([part_spec.reshape(8, rows, width), part_pep.reshape(8, rows, width)], 0)
    parts = parts.astype(jnp.float16)
    parts = lax.all_to_all(parts, AXES, 0, 0, axis_index_groups=core_mp)
    sums = parts.reshape(2, 8, rows, width).astype(jnp.float32).sum(1).reshape(2 * rows, width)
    limits = CLIP_LEVELS * jnp.exp2(-jnp.where(even, exp_spec, exp_pep).astype(jnp.float32))
    q_rows = jnp.clip(sums, -limits, limits).astype(jnp.bfloat16)

    mine = jnp.concatenate([q_rows, teach_rows], 1)
    mine = lax.all_to_all(
        jnp.broadcast_to(mine[None], (16,) + mine.shape), AXES, 0, 0, axis_index_groups=grid
    ).reshape(16 * 2 * rows, -1)
    other = lax.ppermute(mine, AXES, swap)

    acc = pair_grads(mine, other, factor, width).astype(jnp.float16)
    acc = lax.all_to_all(acc.reshape(16, 2 * rows, width), AXES, 0, 0, axis_index_groups=grid)
    acc = factor * acc.astype(jnp.float32).sum(0)
    both = lax.all_gather(acc, AXES, axis=0, axis_index_groups=pairs).reshape(2, 2, rows, width)
    own = lax.dynamic_index_in_dim(both, dp_index % 2, 1, keepdims=False)
    return own[0], own[1]


def solution(mesh):
    groups = device_groups(mesh)

    def run(*args):
        return body(groups, *args)

    in_specs = (
        P("dp", "mp"),
        P("dp", "mp"),
        P("mp", None),
        P("mp", None),
        P("dp", None),
        P(("dp", "mp"), None),
        P(),
        P(),
        P("dp"),
    )
    out_specs = (P(("dp", "mp"), None), P(("dp", "mp"), None))
    return jax.shard_map(run, mesh=mesh, in_specs=in_specs, out_specs=out_specs, check_vma=False)
```

```python
import math

import numpy as np

import jax
import jax.numpy as jnp
from jax import lax
from jax.experimental import pallas as pl
from jax.experimental.pallas import tpu as pltpu
from jax.sharding import PartitionSpec as P

LOGIT_GAIN = 4.0
LOGIT_SHIFT = -2.0
CLIP_LEVELS = 127.0
AXES = ("dp", "mp")


def pair_kernel(factor, width, mine, other, out):
    inner = (((1,), (1,)), ((), ()))
    size = mine.shape[0] // 2
    lane = lax.broadcasted_iota(jnp.int32, (8, 128), 1)
    weigh = jnp.where(lane == 0, 128.0, jnp.where(lane == 1, 1.0, 0.0)).astype(jnp.bfloat16)
    tag_other = lax.dot_general(weigh, other[:, 2 * width :], inner, preferred_element_type=jnp.float32)[0:1]
    targets = []
    for start in (0, size):
        at = pl.ds(start, size)
        teacher = lax.dot_general(
            mine[at, width : 2 * width], other[:, width : 2 * width], inner, preferred_element_type=jnp.float32
        )
        tags = mine[at, 2 * width :].astype(jnp.float32)
        tag_mine = 128.0 * tags[:, 0:1] + tags[:, 1:2]
        hard = jnp.where(tag_mine == tag_other, 0.5, 0.0)
        targets.append(0.25 * jnp.tanh((0.5 * factor) * teacher) - 0.25 + hard)
    for start, target in zip((0, size), targets):
        at = pl.ds(start, size)
        student = lax.dot_general(mine[at, :width], other[:, :width], inner, preferred_element_type=jnp.float32)
        grads = 0.5 * jnp.tanh((0.5 * factor) * student + 0.5 * LOGIT_SHIFT) - target
        out[at, :] = jnp.dot(grads.astype(jnp.bfloat16), other[:, :width], preferred_element_type=jnp.float32)


def pair_grads(mine, other, factor, width):
    return pl.pallas_call(
        lambda *refs: pair_kernel(factor, width, *refs),
        out_shape=jax.ShapeDtypeStruct((mine.shape[0], width), jnp.float32),
        in_specs=[pl.BlockSpec(memory_space=pltpu.VMEM)] * 2,
        out_specs=pl.BlockSpec(memory_space=pltpu.VMEM),
        compiler_params=pltpu.CompilerParams(vmem_limit_bytes=32 * 2**20),
    )(mine, other)


def device_groups(mesh):
    flat = np.arange(mesh.shape["dp"] * mesh.shape["mp"]).reshape(4, 8, 2, 2, 4)
    core_mp = flat.reshape(32, 16)
    flat = flat[..., [0, 1, 3, 2]].reshape(4, 8, 2, 2, 2, 2)
    even = flat[:, :, 0]
    odd = flat[:, :, 1]
    spec_side = even.transpose(1, 3, 0, 2, 4).reshape(16, 16)
    pep_side = odd.transpose(0, 2, 4, 1, 3).reshape(16, 16)
    grid = np.concatenate([spec_side, pep_side], 0)
    pairs = [(int(a), int(b)) for a, b in zip(flat[:, :, 0].ravel(), flat[:, :, 1].ravel())]
    swap = pairs + [(b, a) for a, b in pairs]
    return core_mp.tolist(), grid.tolist(), [list(pair) for pair in pairs], swap


def body(groups, spec_feat, pep_feat, w_spec, w_pep, teach_spec, teach_pep, exp_spec, exp_pep, positive):
    core_mp, grid, pairs, swap = groups
    width = w_spec.shape[1]
    factor = LOGIT_GAIN / math.sqrt(width)
    rows = teach_pep.shape[0]
    dp_index = lax.axis_index("dp")
    mp_index = lax.axis_index("mp")
    even = dp_index % 2 == 0

    tags_spec = lax.dynamic_slice_in_dim(positive, mp_index * rows, rows)
    tags_pep = (dp_index * 8 + mp_index) * rows + jnp.arange(rows, dtype=jnp.int32)

    def with_tags(teach, tags):
        hi = (tags // 128).astype(jnp.bfloat16)[:, None]
        lo = (tags % 128).astype(jnp.bfloat16)[:, None]
        return jnp.concatenate([teach, hi, lo, jnp.zeros((rows, 126), jnp.bfloat16)], 1)

    t_spec = with_tags(lax.dynamic_slice_in_dim(teach_spec, mp_index * rows, rows), tags_spec)
    t_pep = with_tags(teach_pep, tags_pep)
    keep = jnp.where(even, t_spec, t_pep)
    got = lax.ppermute(jnp.where(even, t_pep, t_spec), AXES, swap)
    teach_rows = jnp.concatenate([jnp.where(even, keep, got), jnp.where(even, got, keep)], 0)

    part_spec = jnp.dot(spec_feat, w_spec, preferred_element_type=jnp.float32)
    part_pep = jnp.dot(pep_feat, w_pep, preferred_element_type=jnp.float32)
    part_spec, part_pep = lax.optimization_barrier((part_spec, part_pep))
    parts = jnp.concatenate([part_spec.reshape(8, rows, width), part_pep.reshape(8, rows, width)], 0)
    parts = parts.astype(jnp.float16)
    parts = lax.all_to_all(parts, AXES, 0, 0, axis_index_groups=core_mp)
    sums = parts.reshape(2, 8, rows, width).astype(jnp.float32).sum(1).reshape(2 * rows, width)
    limits = CLIP_LEVELS * jnp.exp2(-jnp.where(even, exp_spec, exp_pep).astype(jnp.float32))
    q_rows = jnp.clip(sums, -limits, limits).astype(jnp.bfloat16)

    mine = jnp.concatenate([q_rows, teach_rows], 1)
    mine = lax.all_to_all(
        jnp.broadcast_to(mine[None], (16,) + mine.shape), AXES, 0, 0, axis_index_groups=grid
    ).reshape(16 * 2 * rows, -1)
    other = lax.ppermute(mine, AXES, swap)

    acc = pair_grads(mine, other, factor, width).astype(jnp.float16)
    acc = lax.all_to_all(acc.reshape(16, 2 * rows, width), AXES, 0, 0, axis_index_groups=grid)
    acc = factor * acc.astype(jnp.float32).sum(0)
    both = lax.all_gather(acc, AXES, axis=0, axis_index_groups=pairs).reshape(2, 2, rows, width)
    return tuple(jnp.where(even, side[0], side[1]) for side in both)


def solution(mesh):
    groups = device_groups(mesh)

    def run(*args):
        return body(groups, *args)

    in_specs = (
        P("dp", "mp"),
        P("dp", "mp"),
        P("mp", None),
        P("mp", None),
        P("dp", None),
        P(("dp", "mp"), None),
        P(),
        P(),
        P("dp"),
    )
    out_specs = (P(("dp", "mp"), None), P(("dp", "mp"), None))
    return jax.shard_map(run, mesh=mesh, in_specs=in_specs, out_specs=out_specs, check_vma=False)
```

```python
import math

import numpy as np

import jax
import jax.numpy as jnp
from jax import lax
from jax.experimental import pallas as pl
from jax.experimental.pallas import tpu as pltpu
from jax.sharding import PartitionSpec as P

LOGIT_GAIN = 4.0
LOGIT_SHIFT = -2.0
CLIP_LEVELS = 127.0
AXES = ("dp", "mp")


def pair_kernel(factor, width, mine, other, out):
    inner = (((1,), (1,)), ((), ()))
    size = mine.shape[0] // 2
    lane = lax.broadcasted_iota(jnp.int32, (8, 128), 1)
    weigh = jnp.where(lane == 0, 128.0, jnp.where(lane == 1, 1.0, 0.0)).astype(jnp.bfloat16)
    tag_other = lax.dot_general(weigh, other[:, 2 * width :], inner, preferred_element_type=jnp.float32)[0:1]
    targets = []
    for start in (0, size):
        at = pl.ds(start, size)
        teacher = lax.dot_general(
            mine[at, width : 2 * width], other[:, width : 2 * width], inner, preferred_element_type=jnp.float32
        )
        tags = mine[at, 2 * width :].astype(jnp.float32)
        tag_mine = 128.0 * tags[:, 0:1] + tags[:, 1:2]
        hard = jnp.where(tag_mine == tag_other, 0.5, 0.0)
        targets.append(0.25 * jnp.tanh((0.5 * factor) * teacher) - 0.25 + hard)
    for start, target in zip((0, size), targets):
        at = pl.ds(start, size)
        student = lax.dot_general(mine[at, :width], other[:, :width], inner, preferred_element_type=jnp.float32)
        grads = 0.5 * jnp.tanh((0.5 * factor) * student + 0.5 * LOGIT_SHIFT) - target
        out[at, :] = jnp.dot(grads.astype(jnp.bfloat16), other[:, :width], preferred_element_type=jnp.float32)


def pair_grads(mine, other, factor, width):
    return pl.pallas_call(
        lambda *refs: pair_kernel(factor, width, *refs),
        out_shape=jax.ShapeDtypeStruct((mine.shape[0], width), jnp.float32),
        in_specs=[pl.BlockSpec(memory_space=pltpu.VMEM)] * 2,
        out_specs=pl.BlockSpec(memory_space=pltpu.VMEM),
        compiler_params=pltpu.CompilerParams(vmem_limit_bytes=32 * 2**20),
    )(mine, other)


def device_groups(mesh):
    flat = np.arange(mesh.shape["dp"] * mesh.shape["mp"]).reshape(4, 8, 2, 2, 4)
    core_mp = flat.reshape(32, 16)
    flat = flat[..., [0, 1, 3, 2]].reshape(4, 8, 2, 2, 2, 2)
    even = flat[:, :, 0]
    odd = flat[:, :, 1]
    spec_side = even.transpose(1, 3, 0, 2, 4).reshape(16, 16)
    pep_side = odd.transpose(0, 2, 4, 1, 3).reshape(16, 16)
    grid = np.concatenate([spec_side, pep_side], 0)
    pairs = [(int(a), int(b)) for a, b in zip(flat[:, :, 0].ravel(), flat[:, :, 1].ravel())]
    swap = pairs + [(b, a) for a, b in pairs]
    return core_mp.tolist(), grid.tolist(), [list(pair) for pair in pairs], swap


def body(groups, spec_feat, pep_feat, w_spec, w_pep, teach_spec, teach_pep, exp_spec, exp_pep, positive):
    core_mp, grid, pairs, swap = groups
    width = w_spec.shape[1]
    factor = LOGIT_GAIN / math.sqrt(width)
    rows = teach_pep.shape[0]
    dp_index = lax.axis_index("dp")
    mp_index = lax.axis_index("mp")
    even = dp_index % 2 == 0

    tags_spec = lax.dynamic_slice_in_dim(positive, mp_index * rows, rows)
    tags_pep = (dp_index * 8 + mp_index) * rows + jnp.arange(rows, dtype=jnp.int32)

    def with_tags(teach, tags):
        hi = (tags // 128).astype(jnp.bfloat16)[:, None]
        lo = (tags % 128).astype(jnp.bfloat16)[:, None]
        return jnp.concatenate([teach, hi, lo, jnp.zeros((rows, 126), jnp.bfloat16)], 1)

    t_spec = with_tags(lax.dynamic_slice_in_dim(teach_spec, mp_index * rows, rows), tags_spec)
    t_pep = with_tags(teach_pep, tags_pep)
    keep = jnp.where(even, t_spec, t_pep)
    got = lax.ppermute(jnp.where(even, t_pep, t_spec), AXES, swap)
    teach_rows = jnp.concatenate([jnp.where(even, keep, got), jnp.where(even, got, keep)], 0)

    parts = lax.dot_general(
        jnp.stack([spec_feat, pep_feat]),
        jnp.stack([w_spec, w_pep]),
        (((2,), (1,)), ((0,), (0,))),
        preferred_element_type=jnp.float32,
    )
    parts = parts.astype(jnp.float16).reshape(16, rows, width)
    parts = lax.all_to_all(parts, AXES, 0, 0, axis_index_groups=core_mp)
    sums = parts.reshape(2, 8, rows, width).astype(jnp.float32).sum(1).reshape(2 * rows, width)
    limits = CLIP_LEVELS * jnp.exp2(-jnp.where(even, exp_spec, exp_pep).astype(jnp.float32))
    q_rows = jnp.clip(sums, -limits, limits).astype(jnp.bfloat16)

    mine = jnp.concatenate([q_rows, teach_rows], 1)
    mine = lax.all_to_all(
        jnp.broadcast_to(mine[None], (16,) + mine.shape), AXES, 0, 0, axis_index_groups=grid
    ).reshape(16 * 2 * rows, -1)
    other = lax.ppermute(mine, AXES, swap)

    acc = pair_grads(mine, other, factor, width).astype(jnp.float16)
    acc = lax.all_to_all(acc.reshape(16, 2 * rows, width), AXES, 0, 0, axis_index_groups=grid)
    acc = factor * acc.astype(jnp.float32).sum(0)
    both = lax.all_gather(acc, AXES, axis=0, axis_index_groups=pairs).reshape(2, 2, rows, width)
    return tuple(jnp.where(even, side[0], side[1]) for side in both)


def solution(mesh):
    groups = device_groups(mesh)

    def run(*args):
        return body(groups, *args)

    in_specs = (
        P("dp", "mp"),
        P("dp", "mp"),
        P("mp", None),
        P("mp", None),
        P("dp", None),
        P(("dp", "mp"), None),
        P(),
        P(),
        P("dp"),
    )
    out_specs = (P(("dp", "mp"), None), P(("dp", "mp"), None))
    return jax.shard_map(run, mesh=mesh, in_specs=in_specs, out_specs=out_specs, check_vma=False)
```

```python
import math

import numpy as np

import jax
import jax.numpy as jnp
from jax import lax
from jax.experimental import pallas as pl
from jax.experimental.pallas import tpu as pltpu
from jax.sharding import PartitionSpec as P

LOGIT_GAIN = 4.0
LOGIT_SHIFT = -2.0
CLIP_LEVELS = 127.0
AXES = ("dp", "mp")


def pair_kernel(factor, width, mine, other, out):
    inner = (((1,), (1,)), ((), ()))
    size = mine.shape[0] // 2
    lane = lax.broadcasted_iota(jnp.int32, (8, 128), 1)
    weigh = jnp.where(lane == 0, 128.0, jnp.where(lane == 1, 1.0, 0.0)).astype(jnp.bfloat16)
    tag_other = lax.dot_general(weigh, other[:, 2 * width :], inner, preferred_element_type=jnp.float32)[0:1]
    targets = []
    for start in (0, size):
        at = pl.ds(start, size)
        teacher = lax.dot_general(
            mine[at, width : 2 * width], other[:, width : 2 * width], inner, preferred_element_type=jnp.float32
        )
        tags = mine[at, 2 * width :].astype(jnp.float32)
        tag_mine = 128.0 * tags[:, 0:1] + tags[:, 1:2]
        hard = jnp.where(tag_mine == tag_other, 0.5, 0.0)
        targets.append(0.25 * jnp.tanh((0.5 * factor) * teacher) - 0.25 + hard)
    for start, target in zip((0, size), targets):
        at = pl.ds(start, size)
        student = lax.dot_general(mine[at, :width], other[:, :width], inner, preferred_element_type=jnp.float32)
        grads = 0.5 * jnp.tanh((0.5 * factor) * student + 0.5 * LOGIT_SHIFT) - target
        out[at, :] = jnp.dot(grads.astype(jnp.bfloat16), other[:, :width], preferred_element_type=jnp.float32)


def pair_grads(mine, other, factor, width):
    return pl.pallas_call(
        lambda *refs: pair_kernel(factor, width, *refs),
        out_shape=jax.ShapeDtypeStruct((mine.shape[0], width), jnp.float32),
        in_specs=[pl.BlockSpec(memory_space=pltpu.VMEM)] * 2,
        out_specs=pl.BlockSpec(memory_space=pltpu.VMEM),
        compiler_params=pltpu.CompilerParams(vmem_limit_bytes=32 * 2**20),
    )(mine, other)


def device_groups(mesh):
    flat = np.arange(mesh.shape["dp"] * mesh.shape["mp"]).reshape(4, 8, 2, 2, 4)
    core_mp = flat.reshape(32, 16)
    flat = flat[..., [0, 1, 3, 2]].reshape(4, 8, 2, 2, 2, 2)
    even = flat[:, :, 0]
    odd = flat[:, :, 1]
    spec_side = even.transpose(1, 4, 3, 0, 2).reshape(16, 16)
    pep_side = odd.transpose(0, 2, 3, 4, 1).reshape(16, 16)
    grid = np.concatenate([spec_side, pep_side], 0)
    pairs = [(int(a), int(b)) for a, b in zip(flat[:, :, 0].ravel(), flat[:, :, 1].ravel())]
    swap = pairs + [(b, a) for a, b in pairs]
    return core_mp.tolist(), grid.tolist(), [list(pair) for pair in pairs], swap


def body(groups, spec_feat, pep_feat, w_spec, w_pep, teach_spec, teach_pep, exp_spec, exp_pep, positive):
    core_mp, grid, pairs, swap = groups
    width = w_spec.shape[1]
    factor = LOGIT_GAIN / math.sqrt(width)
    rows = teach_pep.shape[0]
    dp_index = lax.axis_index("dp")
    mp_index = lax.axis_index("mp")
    even = dp_index % 2 == 0

    tags_spec = lax.dynamic_slice_in_dim(positive, mp_index * rows, rows)
    tags_pep = (dp_index * 8 + mp_index) * rows + jnp.arange(rows, dtype=jnp.int32)

    def with_tags(teach, tags):
        hi = (tags // 128).astype(jnp.bfloat16)[:, None]
        lo = (tags % 128).astype(jnp.bfloat16)[:, None]
        return jnp.concatenate([teach, hi, lo, jnp.zeros((rows, 126), jnp.bfloat16)], 1)

    t_spec = with_tags(lax.dynamic_slice_in_dim(teach_spec, mp_index * rows, rows), tags_spec)
    t_pep = with_tags(teach_pep, tags_pep)
    keep = jnp.where(even, t_spec, t_pep)
    got = lax.ppermute(jnp.where(even, t_pep, t_spec), AXES, swap)
    teach_rows = jnp.concatenate([jnp.where(even, keep, got), jnp.where(even, got, keep)], 0)

    parts = lax.dot_general(
        jnp.stack([spec_feat, pep_feat]),
        jnp.stack([w_spec, w_pep]),
        (((2,), (1,)), ((0,), (0,))),
        preferred_element_type=jnp.float32,
    )
    parts = parts.astype(jnp.float16).reshape(16, rows, width)
    parts = lax.all_to_all(parts, AXES, 0, 0, axis_index_groups=core_mp)
    sums = parts.reshape(2, 8, rows, width).astype(jnp.float32).sum(1).reshape(2 * rows, width)
    limits = CLIP_LEVELS * jnp.exp2(-jnp.where(even, exp_spec, exp_pep).astype(jnp.float32))
    q_rows = jnp.clip(sums, -limits, limits).astype(jnp.bfloat16)

    mine = jnp.concatenate([q_rows, teach_rows], 1)
    mine = lax.all_to_all(
        jnp.broadcast_to(mine[None], (16,) + mine.shape), AXES, 0, 0, axis_index_groups=grid
    ).reshape(16 * 2 * rows, -1)
    other = lax.ppermute(mine, AXES, swap)

    acc = pair_grads(mine, other, factor, width).astype(jnp.float16)
    acc = lax.all_to_all(acc.reshape(16, 2 * rows, width), AXES, 0, 0, axis_index_groups=grid)
    acc = factor * acc.astype(jnp.float32).sum(0)
    both = lax.all_gather(acc, AXES, axis=0, axis_index_groups=pairs).reshape(2, 2, rows, width)
    return tuple(jnp.where(even, side[0], side[1]) for side in both)


def solution(mesh):
    groups = device_groups(mesh)

    def run(*args):
        return body(groups, *args)

    in_specs = (
        P("dp", "mp"),
        P("dp", "mp"),
        P("mp", None),
        P("mp", None),
        P("dp", None),
        P(("dp", "mp"), None),
        P(),
        P(),
        P("dp"),
    )
    out_specs = (P(("dp", "mp"), None), P(("dp", "mp"), None))
    return jax.shard_map(run, mesh=mesh, in_specs=in_specs, out_specs=out_specs, check_vma=False)
```

```python
import math

import numpy as np

import jax
import jax.numpy as jnp
from jax import lax
from jax.experimental import pallas as pl
from jax.experimental.pallas import tpu as pltpu
from jax.sharding import PartitionSpec as P

LOGIT_GAIN = 4.0
LOGIT_SHIFT = -2.0
CLIP_LEVELS = 127.0
PART_SCALE = 256.0
GRAD_SCALE = 64.0
AXES = ("dp", "mp")


def pair_kernel(factor, width, mine, other, out):
    inner = (((1,), (1,)), ((), ()))
    lane = lax.broadcasted_iota(jnp.int32, (8, 128), 1)
    weigh = jnp.where(lane == 0, 128.0, jnp.where(lane == 1, 1.0, 0.0)).astype(jnp.bfloat16)
    tag_other = lax.dot_general(weigh, other[:, 2 * width :], inner, preferred_element_type=jnp.float32)[0:1]
    tags = mine[:, 2 * width :].astype(jnp.float32)
    tag_mine = 128.0 * tags[:, 0:1] + tags[:, 1:2]
    hard = jnp.where(tag_mine == tag_other, 0.5, 0.0)
    teacher = lax.dot_general(
        mine[:, width : 2 * width], other[:, width : 2 * width], inner, preferred_element_type=jnp.float32
    )
    target = 0.25 * jnp.tanh((0.5 * factor) * teacher) - 0.25 + hard
    student = lax.dot_general(mine[:, :width], other[:, :width], inner, preferred_element_type=jnp.float32)
    grads = 0.5 * jnp.tanh((0.5 * factor) * student + 0.5 * LOGIT_SHIFT) - target
    out[...] = jnp.dot(grads.astype(jnp.bfloat16), other[:, :width], preferred_element_type=jnp.float32)


def pair_grads(mine, other, factor, width):
    return pl.pallas_call(
        lambda *refs: pair_kernel(factor, width, *refs),
        out_shape=jax.ShapeDtypeStruct((mine.shape[0], width), jnp.float32),
        in_specs=[pl.BlockSpec(memory_space=pltpu.VMEM)] * 2,
        out_specs=pl.BlockSpec(memory_space=pltpu.VMEM),
        compiler_params=pltpu.CompilerParams(vmem_limit_bytes=32 * 2**20),
    )(mine, other)


def device_groups(mesh):
    flat = np.arange(mesh.shape["dp"] * mesh.shape["mp"]).reshape(4, 8, 2, 2, 4)
    core_mp = flat.reshape(32, 16)
    flat = flat[..., [0, 1, 3, 2]].reshape(4, 8, 2, 2, 2, 2)
    even = flat[:, :, 0]
    odd = flat[:, :, 1]
    spec_side = even.transpose(1, 4, 3, 0, 2).reshape(16, 16)
    pep_side = odd.transpose(0, 2, 3, 4, 1).reshape(16, 16)
    grid = np.concatenate([spec_side, pep_side], 0)
    pairs = [(int(a), int(b)) for a, b in zip(flat[:, :, 0].ravel(), flat[:, :, 1].ravel())]
    swap = pairs + [(b, a) for a, b in pairs]
    return core_mp.tolist(), grid.tolist(), [list(pair) for pair in pairs], swap


def body(groups, spec_feat, pep_feat, w_spec, w_pep, teach_spec, teach_pep, exp_spec, exp_pep, positive):
    core_mp, grid, pairs, swap = groups
    width = w_spec.shape[1]
    factor = LOGIT_GAIN / math.sqrt(width)
    rows = teach_pep.shape[0]
    dp_index = lax.axis_index("dp")
    mp_index = lax.axis_index("mp")
    even = dp_index % 2 == 0

    tags_spec = lax.dynamic_slice_in_dim(positive, mp_index * rows, rows)
    tags_pep = (dp_index * 8 + mp_index) * rows + jnp.arange(rows, dtype=jnp.int32)

    def with_tags(teach, tags):
        hi = (tags // 128).astype(jnp.bfloat16)[:, None]
        lo = (tags % 128).astype(jnp.bfloat16)[:, None]
        return jnp.concatenate([teach, hi, lo, jnp.zeros((rows, 126), jnp.bfloat16)], 1)

    t_spec = with_tags(lax.dynamic_slice_in_dim(teach_spec, mp_index * rows, rows), tags_spec)
    t_pep = with_tags(teach_pep, tags_pep)
    keep = jnp.where(even, t_spec, t_pep)
    got = lax.ppermute(jnp.where(even, t_pep, t_spec), AXES, swap)
    teach_rows = jnp.concatenate([jnp.where(even, keep, got), jnp.where(even, got, keep)], 0)

    parts = lax.dot_general(
        jnp.stack([spec_feat, pep_feat]),
        jnp.stack([w_spec, w_pep]),
        (((2,), (1,)), ((0,), (0,))),
        preferred_element_type=jnp.float32,
    )
    parts = (PART_SCALE * parts).astype(jnp.float16).reshape(16, rows, width)
    parts = lax.all_to_all(parts, AXES, 0, 0, axis_index_groups=core_mp)
    sums = parts.reshape(2, 8, rows, width).astype(jnp.float32).sum(1).reshape(2 * rows, width) * (1.0 / PART_SCALE)
    limits = CLIP_LEVELS * jnp.exp2(-jnp.where(even, exp_spec, exp_pep).astype(jnp.float32))
    q_rows = jnp.clip(sums, -limits, limits).astype(jnp.bfloat16)

    mine = jnp.concatenate([q_rows, teach_rows], 1)
    mine = lax.all_to_all(
        jnp.broadcast_to(mine[None], (16,) + mine.shape), AXES, 0, 0, axis_index_groups=grid
    ).reshape(16 * 2 * rows, -1)
    other = lax.ppermute(mine, AXES, swap)

    acc = (GRAD_SCALE * pair_grads(mine, other, factor, width)).astype(jnp.float16)
    acc = lax.all_to_all(acc.reshape(16, 2 * rows, width), AXES, 0, 0, axis_index_groups=grid)
    acc = (factor / GRAD_SCALE) * acc.astype(jnp.float32).sum(0)
    both = lax.all_gather(acc, AXES, axis=0, axis_index_groups=pairs).reshape(2, 2, rows, width)
    return tuple(jnp.where(even, side[0], side[1]) for side in both)


def solution(mesh):
    groups = device_groups(mesh)

    def run(*args):
        return body(groups, *args)

    in_specs = (
        P("dp", "mp"),
        P("dp", "mp"),
        P("mp", None),
        P("mp", None),
        P("dp", None),
        P(("dp", "mp"), None),
        P(),
        P(),
        P("dp"),
    )
    out_specs = (P(("dp", "mp"), None), P(("dp", "mp"), None))
    return jax.shard_map(run, mesh=mesh, in_specs=in_specs, out_specs=out_specs, check_vma=False)
```

```python
import math

import numpy as np

import jax
import jax.numpy as jnp
from jax import lax
from jax.experimental import pallas as pl
from jax.experimental.pallas import tpu as pltpu
from jax.sharding import PartitionSpec as P

LOGIT_GAIN = 4.0
LOGIT_SHIFT = -2.0
CLIP_LEVELS = 127.0
PART_SCALE = 256.0
GRAD_SCALE = 64.0
AXES = ("dp", "mp")


def pair_kernel(factor, width, mine, other, out):
    inner = (((1,), (1,)), ((), ()))
    lane = lax.broadcasted_iota(jnp.int32, (8, 128), 1)
    weigh = jnp.where(lane == 0, 128.0, jnp.where(lane == 1, 1.0, 0.0)).astype(jnp.bfloat16)
    tag_other = lax.dot_general(weigh, other[:, 2 * width :], inner, preferred_element_type=jnp.float32)[0:1]
    tags = mine[:, 2 * width :].astype(jnp.float32)
    tag_mine = 128.0 * tags[:, 0:1] + tags[:, 1:2]
    hard = jnp.where(tag_mine == tag_other, 0.5, 0.0)
    teacher = lax.dot_general(
        mine[:, width : 2 * width], other[:, width : 2 * width], inner, preferred_element_type=jnp.float32
    )
    target = 0.25 * jnp.tanh((0.5 * factor) * teacher) - 0.25 + hard
    student = lax.dot_general(mine[:, :width], other[:, :width], inner, preferred_element_type=jnp.float32)
    grads = 0.5 * jnp.tanh((0.5 * factor) * student + 0.5 * LOGIT_SHIFT) - target
    out[...] = jnp.dot(grads.astype(jnp.bfloat16), other[:, :width], preferred_element_type=jnp.float32)


def pair_grads(mine, other, factor, width):
    return pl.pallas_call(
        lambda *refs: pair_kernel(factor, width, *refs),
        out_shape=jax.ShapeDtypeStruct((mine.shape[0], width), jnp.float32),
        in_specs=[pl.BlockSpec(memory_space=pltpu.VMEM)] * 2,
        out_specs=pl.BlockSpec(memory_space=pltpu.VMEM),
        compiler_params=pltpu.CompilerParams(vmem_limit_bytes=32 * 2**20),
    )(mine, other)


def device_groups(mesh):
    flat = np.arange(mesh.shape["dp"] * mesh.shape["mp"]).reshape(4, 8, 2, 2, 4)
    core_mp = flat.reshape(32, 16)
    flat = flat[..., [0, 1, 3, 2]].reshape(4, 8, 2, 2, 2, 2)
    even = flat[:, :, 0]
    odd = flat[:, :, 1]
    spec_side = even.transpose(0, 2, 4, 3, 1).reshape(16, 16)
    pep_side = odd.transpose(1, 3, 4, 0, 2).reshape(16, 16)
    grid = np.concatenate([spec_side, pep_side], 0)
    pairs = [(int(a), int(b)) for a, b in zip(flat[:, :, 0].ravel(), flat[:, :, 1].ravel())]
    swap = pairs + [(b, a) for a, b in pairs]
    return core_mp.tolist(), grid.tolist(), [list(pair) for pair in pairs], swap


def body(groups, spec_feat, pep_feat, w_spec, w_pep, teach_spec, teach_pep, exp_spec, exp_pep, positive):
    core_mp, grid, pairs, swap = groups
    width = w_spec.shape[1]
    factor = LOGIT_GAIN / math.sqrt(width)
    rows = teach_pep.shape[0]
    dp_index = lax.axis_index("dp")
    mp_index = lax.axis_index("mp")
    even = dp_index % 2 == 0

    tags_spec = lax.dynamic_slice_in_dim(positive, mp_index * rows, rows)
    tags_pep = (dp_index * 8 + mp_index) * rows + jnp.arange(rows, dtype=jnp.int32)

    def with_tags(teach, tags):
        hi = (tags // 128).astype(jnp.bfloat16)[:, None]
        lo = (tags % 128).astype(jnp.bfloat16)[:, None]
        return jnp.concatenate([teach, hi, lo, jnp.zeros((rows, 126), jnp.bfloat16)], 1)

    t_spec = with_tags(lax.dynamic_slice_in_dim(teach_spec, mp_index * rows, rows), tags_spec)
    t_pep = with_tags(teach_pep, tags_pep)
    keep = jnp.where(even, t_spec, t_pep)
    got = lax.ppermute(jnp.where(even, t_pep, t_spec), AXES, swap)
    teach_rows = jnp.concatenate([jnp.where(even, keep, got), jnp.where(even, got, keep)], 0)

    parts = lax.dot_general(
        jnp.stack([spec_feat, pep_feat]),
        jnp.stack([w_spec, w_pep]),
        (((2,), (1,)), ((0,), (0,))),
        preferred_element_type=jnp.float32,
    )
    parts = (PART_SCALE * parts).astype(jnp.float16).reshape(16, rows, width)
    parts = lax.all_to_all(parts, AXES, 0, 0, axis_index_groups=core_mp)
    sums = parts.reshape(2, 8, rows, width).astype(jnp.float32).sum(1).reshape(2 * rows, width) * (1.0 / PART_SCALE)
    limits = CLIP_LEVELS * jnp.exp2(-jnp.where(even, exp_spec, exp_pep).astype(jnp.float32))
    q_rows = jnp.clip(sums, -limits, limits).astype(jnp.bfloat16)

    mine = jnp.concatenate([q_rows, teach_rows], 1)
    mine = lax.all_to_all(
        jnp.broadcast_to(mine[None], (16,) + mine.shape), AXES, 0, 0, axis_index_groups=grid
    ).reshape(16 * 2 * rows, -1)
    other = lax.ppermute(mine, AXES, swap)

    acc = (GRAD_SCALE * pair_grads(mine, other, factor, width)).astype(jnp.float16)
    acc = lax.all_to_all(acc.reshape(16, 2 * rows, width), AXES, 0, 0, axis_index_groups=grid)
    acc = (factor / GRAD_SCALE) * acc.astype(jnp.float32).sum(0)
    own, foreign = jnp.where(even, acc[:rows], acc[rows:]), jnp.where(even, acc[rows:], acc[:rows])
    both = lax.all_gather(foreign, AXES, axis=0, axis_index_groups=pairs)
    got = jnp.where(even, both[1], both[0])
    return jnp.where(even, own, got), jnp.where(even, got, own)


def solution(mesh):
    groups = device_groups(mesh)

    def run(*args):
        return body(groups, *args)

    in_specs = (
        P("dp", "mp"),
        P("dp", "mp"),
        P("mp", None),
        P("mp", None),
        P("dp", None),
        P(("dp", "mp"), None),
        P(),
        P(),
        P("dp"),
    )
    out_specs = (P(("dp", "mp"), None), P(("dp", "mp"), None))
    return jax.shard_map(run, mesh=mesh, in_specs=in_specs, out_specs=out_specs, check_vma=False)
```

```python
import math

import numpy as np

import jax
import jax.numpy as jnp
from jax import lax
from jax.experimental import pallas as pl
from jax.experimental.pallas import tpu as pltpu
from jax.sharding import PartitionSpec as P

LOGIT_GAIN = 4.0
LOGIT_SHIFT = -2.0
CLIP_LEVELS = 127.0
PART_SCALE = 256.0
GRAD_SCALE = 64.0
AXES = ("dp", "mp")


def pair_kernel(factor, width, mine, other, out):
    inner = (((1,), (1,)), ((), ()))
    lane = lax.broadcasted_iota(jnp.int32, (8, 128), 1)
    weigh = jnp.where(lane == 0, 128.0, jnp.where(lane == 1, 1.0, 0.0)).astype(jnp.bfloat16)
    tag_other = lax.dot_general(weigh, other[:, 2 * width :], inner, preferred_element_type=jnp.float32)[0:1]
    tags = mine[:, 2 * width :].astype(jnp.float32)
    tag_mine = 128.0 * tags[:, 0:1] + tags[:, 1:2]
    hard = jnp.where(tag_mine == tag_other, 0.5, 0.0)
    teacher = lax.dot_general(
        mine[:, width : 2 * width], other[:, width : 2 * width], inner, preferred_element_type=jnp.float32
    )
    target = 0.25 * jnp.tanh((0.5 * factor) * teacher) - 0.25 + hard
    student = lax.dot_general(mine[:, :width], other[:, :width], inner, preferred_element_type=jnp.float32)
    grads = 0.5 * jnp.tanh((0.5 * factor) * student + 0.5 * LOGIT_SHIFT) - target
    out[...] = GRAD_SCALE * jnp.dot(grads.astype(jnp.bfloat16), other[:, :width], preferred_element_type=jnp.float32)


def pair_grads(mine, other, factor, width):
    return pl.pallas_call(
        lambda *refs: pair_kernel(factor, width, *refs),
        out_shape=jax.ShapeDtypeStruct((mine.shape[0], width), jnp.float32),
        in_specs=[pl.BlockSpec(memory_space=pltpu.VMEM)] * 2,
        out_specs=pl.BlockSpec(memory_space=pltpu.VMEM),
        compiler_params=pltpu.CompilerParams(vmem_limit_bytes=32 * 2**20),
    )(mine, other)


def device_groups(mesh):
    flat = np.arange(mesh.shape["dp"] * mesh.shape["mp"]).reshape(4, 8, 2, 2, 4)
    core_mp = flat.reshape(32, 16)
    flat = flat[..., [0, 1, 3, 2]].reshape(4, 8, 2, 2, 2, 2)
    even = flat[:, :, 0]
    odd = flat[:, :, 1]
    spec_side = even.transpose(1, 4, 3, 0, 2).reshape(16, 16)
    pep_side = odd.transpose(0, 2, 3, 4, 1).reshape(16, 16)
    grid = np.concatenate([spec_side, pep_side], 0)
    pairs = [(int(a), int(b)) for a, b in zip(flat[:, :, 0].ravel(), flat[:, :, 1].ravel())]
    swap = pairs + [(b, a) for a, b in pairs]
    return core_mp.tolist(), grid.tolist(), [list(pair) for pair in pairs], swap


def body(groups, spec_feat, pep_feat, w_spec, w_pep, teach_spec, teach_pep, exp_spec, exp_pep, positive):
    core_mp, grid, pairs, swap = groups
    width = w_spec.shape[1]
    factor = LOGIT_GAIN / math.sqrt(width)
    rows = teach_pep.shape[0]
    dp_index = lax.axis_index("dp")
    mp_index = lax.axis_index("mp")
    even = dp_index % 2 == 0

    tags_spec = lax.dynamic_slice_in_dim(positive, mp_index * rows, rows)
    tags_pep = (dp_index * 8 + mp_index) * rows + jnp.arange(rows, dtype=jnp.int32)

    def with_tags(teach, tags):
        hi = (tags // 128).astype(jnp.bfloat16)[:, None]
        lo = (tags % 128).astype(jnp.bfloat16)[:, None]
        return jnp.concatenate([teach, hi, lo, jnp.zeros((rows, 126), jnp.bfloat16)], 1)

    t_spec = with_tags(lax.dynamic_slice_in_dim(teach_spec, mp_index * rows, rows), tags_spec)
    t_pep = with_tags(teach_pep, tags_pep)
    keep = jnp.where(even, t_spec, t_pep)
    got = lax.ppermute(jnp.where(even, t_pep, t_spec), AXES, swap)
    teach_rows = jnp.concatenate([jnp.where(even, keep, got), jnp.where(even, got, keep)], 0)

    parts = lax.dot_general(
        jnp.stack([spec_feat, pep_feat]),
        jnp.stack([w_spec, w_pep]),
        (((2,), (1,)), ((0,), (0,))),
        preferred_element_type=jnp.float32,
    )
    parts = (PART_SCALE * parts).astype(jnp.float16).reshape(16, rows, width)
    parts = lax.all_to_all(parts, AXES, 0, 0, axis_index_groups=core_mp)
    sums = parts.reshape(2, 8, rows, width).astype(jnp.float32).sum(1).reshape(2 * rows, width) * (1.0 / PART_SCALE)
    limits = CLIP_LEVELS * jnp.exp2(-jnp.where(even, exp_spec, exp_pep).astype(jnp.float32))
    q_rows = jnp.clip(sums, -limits, limits).astype(jnp.bfloat16)

    mine = jnp.concatenate([q_rows, teach_rows], 1)
    mine = lax.all_to_all(
        jnp.broadcast_to(mine[None], (16,) + mine.shape), AXES, 0, 0, axis_index_groups=grid
    ).reshape(16 * 2 * rows, -1)
    other = lax.ppermute(mine, AXES, swap)

    acc = pair_grads(mine, other, factor, width).astype(jnp.float16)
    acc = lax.all_to_all(acc.reshape(16, 2 * rows, width), AXES, 0, 0, axis_index_groups=grid)
    acc = (factor / GRAD_SCALE) * acc.astype(jnp.float32).sum(0)
    own, foreign = jnp.where(even, acc[:rows], acc[rows:]), jnp.where(even, acc[rows:], acc[:rows])
    both = lax.all_gather(foreign, AXES, axis=0, axis_index_groups=pairs)
    got = jnp.where(even, both[1], both[0])
    return jnp.where(even, own, got), jnp.where(even, got, own)


def solution(mesh):
    groups = device_groups(mesh)

    def run(*args):
        return body(groups, *args)

    in_specs = (
        P("dp", "mp"),
        P("dp", "mp"),
        P("mp", None),
        P("mp", None),
        P("dp", None),
        P(("dp", "mp"), None),
        P(),
        P(),
        P("dp"),
    )
    out_specs = (P(("dp", "mp"), None), P(("dp", "mp"), None))
    return jax.shard_map(run, mesh=mesh, in_specs=in_specs, out_specs=out_specs, check_vma=False)
```
